32 devices in a mesh: span: 16 (over z, y, core), head: 2 (over x).
Axes of the slice: x: 2, y: 2, z: 4, core: 2. Of those that a mesh axis runs over, the one named last changes fastest.
Arguments:
- queries: bfloat16 [8192, 6144], P('span', 'head'), may hold values from -16 to 16
- stacked_key_vectors: bfloat16 [8192, 1024], P('span', 'head'), may hold values from -16 to 16
- stacked_value_vectors: bfloat16 [8192, 1024], P('span', 'head'), may hold values from -6 to 6
- out_weight: bfloat16 [6144, 6144], P('head'), may hold values from -0.625 to 0.625
- residual: bfloat16 [8192, 6144], P(('span', 'head')), may hold values from -6 to 6
- gate_table: float32 [32, 6144], replicated, may hold values from 0.25 to 1.75
- noise_step: int32 [16], replicated, may hold values from 0 to 31
- older_count: int32 [16], replicated, may hold values from 0 to 7, as said below
Outputs:
- output: bfloat16 [8192, 6144], P(('span', 'head'))
The draws below stay inside these ranges and needn't reach their ends.
Inputs may be any that keep to these rules, and one draw needn't show every extreme that they name: older_count[c] is at most c; some span has exactly 7.
All inputs are finite; a program needn't handle non-finite values.
Results may differ from the reference program's by a relative error of at most 0.014.
Values may be sent and summed in bfloat16 or wider, within the bound.
No kernel may reach another device: no remote copies, remote signals or barrier semaphores. Data moves between devices by JAX's collectives and lax.ppermute only.
A program may use at most 192 MiB of HBM per device.

```python
import math
import jax
import jax.numpy as jnp
from jax import lax

D = 6144
QUERY_HEADS = 48
KEY_VALUE_HEADS = 8
HEAD_SIZE = 128
SPAN_TOKENS = 512
OLDER_SPAN_LIMIT = 7
STEPS = 32
SPANS = 16
WINDOW_TOKENS = 8192
N_HEAD = 2


def draw_queries(key, part):
    base_offset = 2.0 * jnp.clip(jax.random.normal(jax.random.fold_in(key, 11), (WINDOW_TOKENS, QUERY_HEADS, HEAD_SIZE), jnp.float32), -4.0, 4.0)
    return base_offset.reshape(WINDOW_TOKENS, QUERY_HEADS * HEAD_SIZE).astype(jnp.bfloat16)


def draw_stacked_key_vectors(key, part):
    base_offset = jnp.clip(jax.random.normal(jax.random.fold_in(key, 13), (WINDOW_TOKENS, KEY_VALUE_HEADS, HEAD_SIZE), jnp.float32), -4.0, 4.0)
    return base_offset.reshape(WINDOW_TOKENS, KEY_VALUE_HEADS * HEAD_SIZE).astype(jnp.bfloat16)


def draw_older_count(key, part):
    drawn = jax.random.randint(jax.random.fold_in(key, 21), (SPANS,), 0, OLDER_SPAN_LIMIT + 1)
    span_ids = jnp.arange(SPANS, dtype=jnp.int32)
    drawn = jnp.minimum(drawn, span_ids)
    picked = jax.random.randint(jax.random.fold_in(key, 22), (), OLDER_SPAN_LIMIT, SPANS)
    drawn = jnp.where(span_ids == picked, OLDER_SPAN_LIMIT, drawn)
    return drawn.astype(jnp.int32)


def plant(values, rng, low, high):
    index_at = [jax.random.randint(jax.random.fold_in(rng, axis), (), 0, length) for axis, length in enumerate(values.shape)]
    main_axis = values.shape.index(max(values.shape))
    beside = index_at[:main_axis] + [(index_at[main_axis] + 1) % values.shape[main_axis]] + index_at[main_axis + 1:]
    return values.at[tuple(index_at)].set(low).at[tuple(beside)].set(high)


def shard_levels(stream_key, extent, pieces, low, largest):
    gain, own = 1.0, jax.random.fold_in(stream_key, 6)
    for axis_at, blocks in pieces:
        draws = jnp.exp(jax.random.uniform(jax.random.fold_in(own, axis_at), (blocks,), jnp.float32, low / len(pieces), largest / len(pieces)))
        gain = gain * jnp.repeat(draws, extent[axis_at] // blocks).reshape([-1 if axis == axis_at else 1 for axis in range(len(extent))])
    return gain


def scatter_about(key, extent, spread, limit, cuts=(), kind=jnp.bfloat16):
    entries = jax.random.normal(key, extent, jnp.float32) * spread
    if len(cuts) > 0:
        entries = shard_levels(key, extent, cuts, -0.22, 0.18) * entries
    return jnp.clip(entries, min=-limit, max=limit).astype(kind)


def setup_inputs(seed: int = 0) -> dict:
    arg_keys = jax.random.split(jax.random.key(seed), 9)
    queries = draw_queries(jax.random.fold_in(arg_keys[8], 71), 0)
    stacked_key_vectors = draw_stacked_key_vectors(jax.random.fold_in(arg_keys[8], 71), 0)
    stacked_value_vectors = scatter_about(arg_keys[2], (WINDOW_TOKENS, KEY_VALUE_HEADS * HEAD_SIZE), 1.0, 6.0, ((0, 16), (1, 2)))
    out_weight = scatter_about(arg_keys[3], (QUERY_HEADS * HEAD_SIZE, D), (QUERY_HEADS * HEAD_SIZE // 64) ** -0.5, 0.625, ((0, 2),))
    residual = scatter_about(arg_keys[4], (WINDOW_TOKENS, D), 1.0, 6.0, ((0, 32),))
    gate_table = jnp.clip(jax.random.uniform(arg_keys[5], (STEPS, D), jnp.float32, 0.25, 1.75), 0.25, 1.75)
    noise_step = plant(jax.random.randint(arg_keys[6], (SPANS,), 0, STEPS), jax.random.fold_in(arg_keys[6], 1), 0, STEPS - 1).astype(jnp.int32)
    older_count = draw_older_count(jax.random.fold_in(arg_keys[8], 71), 0)
    return {"queries": queries, "stacked_key_vectors": stacked_key_vectors, "stacked_value_vectors": stacked_value_vectors, "out_weight": out_weight, "residual": residual, "gate_table": gate_table, "noise_step": noise_step, "older_count": older_count}


def reference(queries, stacked_key_vectors, stacked_value_vectors, out_weight, residual, gate_table, noise_step, older_count):
    window_length = OLDER_SPAN_LIMIT + 1
    query_group_size = QUERY_HEADS // KEY_VALUE_HEADS
    width_head = QUERY_HEADS * HEAD_SIZE // N_HEAD
    pad_amount = jnp.zeros((OLDER_SPAN_LIMIT * SPAN_TOKENS, KEY_VALUE_HEADS * HEAD_SIZE), stacked_key_vectors.dtype)
    padded_keys = jnp.concatenate([pad_amount, stacked_key_vectors], axis=0)
    padded_values = jnp.concatenate([pad_amount, stacked_value_vectors], axis=0)
    weight_groups = out_weight.astype(jnp.float32).reshape(N_HEAD, width_head, D)

    def one_span(span_idx):
        starting_row = (span_idx * SPAN_TOKENS).astype(jnp.int32)
        query_span_rows = lax.dynamic_slice_in_dim(queries, starting_row, SPAN_TOKENS, 0).reshape(SPAN_TOKENS, KEY_VALUE_HEADS, query_group_size, HEAD_SIZE)
        key_row_block = lax.dynamic_slice_in_dim(padded_keys, starting_row, window_length * SPAN_TOKENS, 0).reshape(window_length * SPAN_TOKENS, KEY_VALUE_HEADS, HEAD_SIZE)
        value_row_block = lax.dynamic_slice_in_dim(padded_values, starting_row, window_length * SPAN_TOKENS, 0).reshape(window_length * SPAN_TOKENS, KEY_VALUE_HEADS, HEAD_SIZE)
        block_of = jnp.arange(window_length * SPAN_TOKENS, dtype=jnp.int32) // SPAN_TOKENS
        distance = OLDER_SPAN_LIMIT - block_of
        visible = distance <= older_count[span_idx]

        def single_head(head_idx):
            head_queries = query_span_rows[:, head_idx].astype(jnp.float32)
            head_keys = key_row_block[:, head_idx].astype(jnp.float32)
            head_values = value_row_block[:, head_idx].astype(jnp.float32)
            scores = jnp.einsum('trd,ud->rtu', head_queries, head_keys) / math.sqrt(HEAD_SIZE)
            masked = jnp.where(visible[None, None, :], scores, -1e+30)
            row_max = lax.optimization_barrier(jnp.max(masked, axis=-1))
            weights = jnp.where(visible[None, None, :], jnp.exp(masked - row_max[..., None]), 0.0)
            row_total = lax.optimization_barrier(jnp.sum(weights, axis=-1))
            rounded = lax.optimization_barrier(weights.astype(jnp.bfloat16)).astype(jnp.float32)
            numerator = jnp.einsum('rtu,ud->rtd', rounded, head_values)
            return (numerator / row_total[..., None]).astype(jnp.bfloat16)
        head_outputs = lax.map(single_head, jnp.arange(KEY_VALUE_HEADS, dtype=jnp.int32))
        attention = head_outputs.transpose(2, 0, 1, 3).reshape(SPAN_TOKENS, QUERY_HEADS * HEAD_SIZE)
        partials = jnp.einsum('tnf,nfd->ntd', attention.astype(jnp.float32).reshape(SPAN_TOKENS, N_HEAD, width_head), weight_groups)
        partials = lax.optimization_barrier(partials.astype(jnp.bfloat16)).astype(jnp.float32)
        projected = lax.optimization_barrier(jnp.sum(partials, axis=0))
        gate_row = gate_table[noise_step[span_idx]]
        residual_rows = lax.dynamic_slice_in_dim(residual, starting_row, SPAN_TOKENS, 0).astype(jnp.float32)
        return (residual_rows + gate_row[None, :] * projected).astype(jnp.bfloat16)
    result = lax.map(one_span, jnp.arange(SPANS, dtype=jnp.int32))
    return result.reshape(WINDOW_TOKENS, D)
```

```python
import functools
import math

import jax
import jax.numpy as jnp
from jax import lax
from jax.experimental import pallas as pl
from jax.experimental.pallas import tpu as pltpu
from jax.sharding import PartitionSpec as P

HEAD_SIZE = 128
MAX_BLOCKS = 8
EXPONENT_SCALE = math.log2(math.e) / math.sqrt(HEAD_SIZE)
TOTAL_LIMIT = 2.0**100
F32 = jnp.float32
BF16 = jnp.bfloat16
NT = (((1,), (1,)), ((), ()))


def attention_kernel(n_slot, rows, group, sub, meta, q_ref, *rest):
    kv_refs = rest[:n_slot]
    out_ref, keys, values, scaled, acc, top = rest[n_slot:]
    span = kv_refs[0].shape[1]
    count = jnp.int32(0)
    for j in range(n_slot):
        at = count

        def pack(at=at, j=j):
            key_block = kv_refs[j][0]
            keys[at, :, :HEAD_SIZE] = key_block
            keys[at, :, HEAD_SIZE:] = key_block
            values[at, :, :HEAD_SIZE] = kv_refs[j][1]
            values[at, :, HEAD_SIZE:] = jnp.ones((span, HEAD_SIZE), BF16)

        if j == 0:
            pack()
            count = jnp.int32(1)
        else:
            pl.when(meta[j] > 0)(pack)
            count = count + jnp.where(meta[j] > 0, 1, 0).astype(jnp.int32)
    for h in range(group):
        q = q_ref[:, h * HEAD_SIZE : (h + 1) * HEAD_SIZE].astype(F32) * EXPONENT_SCALE
        high = q.astype(BF16)
        scaled[h * rows : (h + 1) * rows, :HEAD_SIZE] = high
        scaled[h * rows : (h + 1) * rows, HEAD_SIZE:] = (q - high.astype(F32)).astype(BF16)
    n_sub = group * rows // sub

    def scores(at, block):
        return lax.dot_general(scaled[at, :], keys[block], NT, preferred_element_type=F32)

    def weigh(p, block):
        return jnp.dot(p.astype(BF16), values[block], preferred_element_type=F32)

    for i in range(n_sub):
        at = pl.ds(i * sub, sub)
        s = scores(at, 0)
        row_top = jnp.max(s, axis=1, keepdims=True)
        top[at, :] = jnp.broadcast_to(row_top, (sub, HEAD_SIZE))
        acc[at, :] = weigh(jnp.exp2(s - row_top), 0)

    def older(block, carry):
        for i in range(n_sub):
            at = pl.ds(i * sub, sub)
            acc[at, :] += weigh(jnp.exp2(scores(at, block) - top[at, :1]), block)
        return carry

    lax.fori_loop(1, count, older, 0)

    @pl.when(jnp.logical_not(jnp.max(acc[:, HEAD_SIZE:]) < TOTAL_LIMIT))
    def _():
        def again(i, carry):
            at = pl.ds(pl.multiple_of(i * sub, sub), sub)
            acc[at, :] = jnp.zeros((sub, 2 * HEAD_SIZE), F32)
            top[at, :] = jnp.full((sub, HEAD_SIZE), -1e30, F32)

            def block_step(block, inner):
                s = scores(at, block)
                old_top = top[at, :1]
                new_top = jnp.maximum(old_top, jnp.max(s, axis=1, keepdims=True))
                top[at, :] = jnp.broadcast_to(new_top, (sub, HEAD_SIZE))
                acc[at, :] = acc[at, :] * jnp.exp2(old_top - new_top) + weigh(jnp.exp2(s - new_top), block)
                return inner

            return lax.fori_loop(0, count, block_step, carry)

        lax.fori_loop(0, n_sub, again, 0)

    for h in range(group):
        at = pl.ds(h * rows, rows)
        out_ref[:, h * HEAD_SIZE : (h + 1) * HEAD_SIZE] = (acc[at, :HEAD_SIZE] / acc[at, HEAD_SIZE:]).astype(BF16)


def attention(queries, blocks, visible, row_block, rows, group, head, lane):
    n_slot = len(blocks)
    span = blocks[0].shape[1]
    width = group * HEAD_SIZE
    meta = jnp.concatenate([row_block[None], visible[1:]]).astype(jnp.int32)
    work = group * rows * 5 * span * HEAD_SIZE
    return pl.pallas_call(
        functools.partial(attention_kernel, n_slot, rows, group, min(rows, 256)),
        out_shape=jax.ShapeDtypeStruct((rows, width), BF16),
        grid_spec=pltpu.PrefetchScalarGridSpec(
            num_scalar_prefetch=1,
            grid=(1,),
            in_specs=[pl.BlockSpec((rows, width), lambda i, m: (m[0], head))]
            + [pl.BlockSpec((2, span, HEAD_SIZE), lambda i, m: (0, 0, lane))] * n_slot,
            out_specs=pl.BlockSpec((rows, width), lambda i, m: (0, 0)),
            scratch_shapes=[
                pltpu.VMEM((MAX_BLOCKS, span, 2 * HEAD_SIZE), BF16),
                pltpu.VMEM((MAX_BLOCKS, span, 2 * HEAD_SIZE), BF16),
                pltpu.VMEM((group * rows, 2 * HEAD_SIZE), BF16),
                pltpu.VMEM((group * rows, 2 * HEAD_SIZE), F32),
                pltpu.VMEM((group * rows, HEAD_SIZE), F32),
            ],
        ),
        compiler_params=pltpu.CompilerParams(vmem_limit_bytes=40 * 2**20),
        cost_estimate=pl.CostEstimate(flops=8 * work, bytes_accessed=4 * 2**20, transcendentals=0),
    )(meta, queries, *blocks)


def gather_blocks(own, n_span):
    def move(block, sends, target):
        route = [(i, target(i)) for i in range(n_span) if sends(i) and 0 <= target(i) < n_span]
        return lax.ppermute(block, "span", route)

    def up(i):
        return i + 4

    def across(i):
        return i ^ 2

    def beside(i):
        return i ^ 1

    def always(i):
        return True

    a1 = move(own, always, up)
    y0 = move(own, lambda i: i & 2 == 0, across)
    c0 = move(own, lambda i: i & 1 == 0, beside)
    a1y = move(a1, always, across)
    a2 = move(a1, lambda i: i & 3 > 0, up)
    y0c = move(y0, lambda i: i & 2 > 0, beside)
    a1c = move(a1, always, beside)
    a1yc = move(a1y, always, beside)
    a2y = move(a2, lambda i: i & 2 > 0, across)
    a2c = move(a2, lambda i: i & 1 > 0, beside)
    a2yc = move(a2y, lambda i: i & 2 == 0, beside)
    return [own, c0, y0, y0c, a1, a1c, a1y, a1yc, a2, a2c, a2y, a2yc]


def on_device(
    queries,
    stacked_key_vectors,
    stacked_value_vectors,
    out_weight,
    residual,
    gate_table,
    noise_step,
    older_count,
):
    span_len = queries.shape[0]
    kv_heads = stacked_key_vectors.shape[1] // HEAD_SIZE
    group = queries.shape[1] // HEAD_SIZE // kv_heads
    model_width = out_weight.shape[1]
    n_span = lax.axis_size("span")
    n_head = lax.axis_size("head")
    my_span = lax.axis_index("span")
    my_head = lax.axis_index("head")
    older_mine = older_count[my_span]
    rows = span_len // n_head

    sources = [(my_span - 4 * (j // 4)) ^ (j % 4) for j in range(12)]
    distances = [my_span - source for source in sources]
    visible = jnp.stack([(d >= 0) & (d <= older_mine) for d in distances]).astype(jnp.int32)

    n_chunk = 2 if kv_heads % 2 == 0 else 1
    per_chunk = kv_heads // n_chunk
    gathered = []
    for c in range(n_chunk):
        at = slice(c * per_chunk * HEAD_SIZE, (c + 1) * per_chunk * HEAD_SIZE)
        gathered.append(gather_blocks(jnp.stack([stacked_key_vectors[:, at], stacked_value_vectors[:, at]]), n_span))

    def attend(row_block):
        pieces = []
        for head in range(kv_heads):
            blocks = gathered[head // per_chunk]
            pieces.append(attention(queries, blocks, visible, row_block, rows, group, head, head % per_chunk))
        return jnp.concatenate(pieces, axis=1)

    n_column = 4
    columns = model_width // n_column

    def project(attended, c):
        weight = out_weight[:, c * columns : (c + 1) * columns]
        return jnp.dot(attended, weight, preferred_element_type=F32)

    received = [[] for _ in range(n_column)]
    for k in range(1, n_head):
        attended = attend((my_head + k) % n_head)
        route = [(i, (i + k) % n_head) for i in range(n_head)]
        for c in range(n_column):
            received[c].append(lax.ppermute(project(attended, c).astype(BF16), "head", route))

    attended = attend(my_head)
    gate_row = lax.dynamic_slice_in_dim(gate_table, noise_step[my_span], 1, 0)
    outs = []
    for c in range(n_column):
        at = slice(c * columns, (c + 1) * columns)
        total = project(attended, c)
        for part in received[c]:
            total = total + part.astype(F32)
        outs.append((residual[:, at].astype(F32) + gate_row[:, at] * total).astype(BF16))
    return jnp.concatenate(outs, axis=1)


def solution(mesh):
    in_specs = (
        P("span", "head"),
        P("span", "head"),
        P("span", "head"),
        P("head", None),
        P(("span", "head"), None),
        P(),
        P(),
        P(),
    )
    out_specs = P(("span", "head"), None)
    return jax.shard_map(
        on_device, mesh=mesh, in_specs=in_specs, out_specs=out_specs, check_vma=False
    )
```

```python
import functools
import math

import jax
import jax.numpy as jnp
from jax import lax
from jax.experimental import pallas as pl
from jax.experimental.pallas import tpu as pltpu
from jax.sharding import PartitionSpec as P

HEAD_SIZE = 128
MAX_BLOCKS = 8
EXPONENT_SCALE = math.log2(math.e) / math.sqrt(HEAD_SIZE)
TOTAL_LIMIT = 2.0**100
F32 = jnp.float32
BF16 = jnp.bfloat16
NT = (((1,), (1,)), ((), ()))


def slot_source(slot, my_span):
    core, y = my_span & 1, (my_span >> 1) & 1
    plane = my_span - 4
    return [
        (my_span, y >= 0),
        (my_span ^ 1, core == 1),
        (my_span ^ 2, y == 1),
        (my_span ^ 3, y == 1),
        (plane, y >= 0),
        (plane ^ 1, y >= 0),
        (plane ^ 2, y == 0),
        (plane ^ 3, y == 0),
        (plane ^ 2, y == 1),
        (plane ^ 3, y == 1),
        (my_span - 7, core == 0),
        (my_span - 6, y == 0),
        ((my_span - 6) ^ 1, y == 0),
    ][slot]


def attention_kernel(slots, rows, group, sub, first, last, place, older_count, q_ref, *rest):
    kv_refs, rest = rest[: len(slots)], rest[len(slots) :]
    if not first:
        (sum_in, mark_in), rest = rest[:2], rest[2:]
    if last:
        weight_ref, out_ref, product_ref, keys, values, scaled, acc, mark, attended, near_weight, arrived = rest
        load = pltpu.make_async_copy(weight_ref.at[:, pl.ds(0, near_weight.shape[1])], near_weight, arrived)
        pl.when(pl.program_id(0) == 0)(load.start)
    else:
        sum_out, mark, keys, values, scaled, acc = rest
    half = HEAD_SIZE // 2
    span = kv_refs[0].shape[1]
    my_span = place[1]
    older_mine = older_count[my_span]

    def pack(at, j):
        key_block = kv_refs[j][0]
        keys[at, :, :HEAD_SIZE] = key_block
        keys[at, :, HEAD_SIZE:] = key_block
        values[at, :, :HEAD_SIZE] = kv_refs[j][1]
        values[at, :, HEAD_SIZE:] = jnp.ones((span, HEAD_SIZE), BF16)

    count = jnp.int32(0)
    for j, slot in enumerate(slots):
        if slot == 0:
            pack(0, 0)
            count = jnp.int32(1)
        else:
            source, used = slot_source(slot, my_span)
            seen = used & (source < my_span) & (my_span - source <= older_mine)
            pl.when(seen)(functools.partial(pack, count, j))
            count = count + jnp.where(seen, 1, 0).astype(jnp.int32)

    def scale():
        for h in range(group):
            q = q_ref[:, h * HEAD_SIZE : (h + 1) * HEAD_SIZE].astype(F32) * EXPONENT_SCALE
            high = q.astype(BF16)
            scaled[h * rows : (h + 1) * rows, :HEAD_SIZE] = high
            scaled[h * rows : (h + 1) * rows, HEAD_SIZE:] = (q - high.astype(F32)).astype(BF16)

    n_sub = group * rows // sub

    def scores(at, block):
        return lax.dot_general(scaled[at, :], keys[block], NT, preferred_element_type=F32)

    def weigh(p, block):
        return jnp.dot(p.astype(BF16), values[block], preferred_element_type=F32)

    if first:
        scale()
        mark[:, :half] = jnp.zeros((group * rows, half), F32)
        for i in range(n_sub):
            at = pl.ds(i * sub, sub)
            s = scores(at, 0)
            row_top = jnp.max(s, axis=1, keepdims=True)
            mark[at, half:] = jnp.broadcast_to(row_top, (sub, half))
            acc[at, :] = weigh(jnp.exp2(s - row_top), 0)
    else:
        pl.when(count > 0)(scale)
        acc[:, :HEAD_SIZE] = sum_in[...]
        acc[:, HEAD_SIZE:] = jnp.zeros((group * rows, HEAD_SIZE), F32)
        mark[...] = mark_in[...]

    def add_block(block):
        for i in range(n_sub):
            at = pl.ds(i * sub, sub)
            acc[at, :] += weigh(jnp.exp2(scores(at, block) - mark[at, half : half + 1]), block)

    begin = 1 if first else 0
    if len(slots) > begin:
        pairs = (count - begin) // 2

        def two_blocks(i, carry):
            add_block(begin + 2 * i)
            add_block(begin + 2 * i + 1)
            return carry

        lax.fori_loop(0, pairs, two_blocks, 0)
        pl.when(begin + 2 * pairs < count)(functools.partial(add_block, count - 1))

        @pl.when(jnp.logical_not(jnp.max(acc[:, HEAD_SIZE:]) < TOTAL_LIMIT))
        def _():
            def again(i, carry):
                at = pl.ds(pl.multiple_of(i * sub, sub), sub)
                acc[at, :] = jnp.zeros((sub, 2 * HEAD_SIZE), F32)
                if first:
                    mark[at, half:] = jnp.full((sub, half), -1e30, F32)
                else:
                    acc[at, :HEAD_SIZE] = sum_in[at, :]
                    mark[at, :] = mark_in[at, :]

                def block_step(block, inner):
                    s = scores(at, block)
                    old_top = mark[at, half : half + 1]
                    new_top = jnp.maximum(old_top, jnp.max(s, axis=1, keepdims=True))
                    shrink = jnp.exp2(old_top - new_top)
                    mark[at, :half] = mark[at, :half] * shrink
                    mark[at, half:] = jnp.broadcast_to(new_top, (sub, half))
                    acc[at, :] = acc[at, :] * shrink + weigh(jnp.exp2(s - new_top), block)
                    return inner

                return lax.fori_loop(0, count, block_step, carry)

            lax.fori_loop(0, n_sub, again, 0)

    if not last:
        mark[:, :half] += acc[:, HEAD_SIZE : HEAD_SIZE + half]
        sum_out[...] = acc[:, :HEAD_SIZE]
        return
    head = pl.program_id(0)
    for h in range(group):
        at = pl.ds(h * rows, rows)
        total = acc[at, HEAD_SIZE:] + mark[at, :1]
        result = (acc[at, :HEAD_SIZE] / total).astype(BF16)
        out_ref[:, h * HEAD_SIZE : (h + 1) * HEAD_SIZE] = result
        here = (head * group + h) * HEAD_SIZE
        attended[:, pl.ds(pl.multiple_of(here, HEAD_SIZE), HEAD_SIZE)] = result

    @pl.when(head == pl.num_programs(0) - 1)
    def _():
        load.wait()
        tile = 512
        for begin in range(0, product_ref.shape[1], tile):
            at = slice(begin, begin + tile)
            product = jnp.dot(attended[...], near_weight[:, at], preferred_element_type=F32)
            product_ref[:, at] = product.astype(BF16)


def attention(queries, place, older_count, rows, group, blocks, state=None, weight=None, columns=0):
    slots = sorted(blocks)
    arrays = [blocks[slot] for slot in slots]
    first = state is None
    last = weight is not None
    kv_heads = arrays[0].shape[2] // HEAD_SIZE
    span = arrays[0].shape[1]
    width = group * HEAD_SIZE
    all_rows = group * rows
    n_block = min(MAX_BLOCKS, len(arrays))
    state_spec = pl.BlockSpec((None, all_rows, HEAD_SIZE), lambda g, p, o: (g, 0, 0))
    in_specs = [pl.BlockSpec((rows, width), lambda g, p, o: (p[0], g))]
    in_specs += [pl.BlockSpec((2, span, HEAD_SIZE), lambda g, p, o: (0, 0, g))] * len(arrays)
    scratch = [
        pltpu.VMEM((n_block, span, 2 * HEAD_SIZE), BF16),
        pltpu.VMEM((n_block, span, 2 * HEAD_SIZE), BF16),
        pltpu.VMEM((all_rows, 2 * HEAD_SIZE), BF16),
        pltpu.VMEM((all_rows, 2 * HEAD_SIZE), F32),
    ]
    if not first:
        in_specs += [state_spec, state_spec]
        arrays += list(state)
    if last:
        in_specs.append(pl.BlockSpec(memory_space=pl.ANY))
        arrays.append(weight)
        out_shape = [
            jax.ShapeDtypeStruct((rows, kv_heads * width), BF16),
            jax.ShapeDtypeStruct((rows, columns), BF16),
        ]
        out_specs = [
            pl.BlockSpec((rows, width), lambda g, p, o: (0, g)),
            pl.BlockSpec((rows, columns), lambda g, p, o: (0, 0)),
        ]
        scratch += [
            pltpu.VMEM((all_rows, HEAD_SIZE), F32),
            pltpu.VMEM((rows, kv_heads * width), BF16),
            pltpu.VMEM((weight.shape[0], columns), BF16),
            pltpu.SemaphoreType.DMA,
        ]
    else:
        out_shape = [pltpu.HBM((kv_heads, all_rows, HEAD_SIZE), F32)] * 2
        out_specs = [state_spec, state_spec]
    return pl.pallas_call(
        functools.partial(attention_kernel, slots, rows, group, min(rows, 256), first, last),
        out_shape=out_shape,
        grid_spec=pltpu.PrefetchScalarGridSpec(
            num_scalar_prefetch=2,
            grid=(kv_heads,),
            in_specs=in_specs,
            out_specs=out_specs,
            scratch_shapes=scratch,
        ),
        compiler_params=pltpu.CompilerParams(vmem_limit_bytes=48 * 2**20),
    )(place, older_count, queries, *arrays)


def project_kernel(n_part, a_ref, w_ref, *rest):
    total = jnp.dot(a_ref[...], w_ref[...], preferred_element_type=F32)
    if n_part == 0:
        rest[0][...] = total.astype(BF16)
        return
    gate_ref, residual_ref = rest[:2]
    for part in rest[2 : 2 + n_part]:
        total = total + part[...].astype(F32)
    rest[-1][...] = (residual_ref[...].astype(F32) + gate_ref[...] * total).astype(BF16)


def combine_kernel(n_part, gate_ref, residual_ref, *rest):
    total = rest[0][...].astype(F32)
    for part in rest[1:n_part]:
        total = total + part[...].astype(F32)
    rest[-1][...] = (residual_ref[...].astype(F32) + gate_ref[...] * total).astype(BF16)


def project(attended, weight, begin, columns, tile):
    rows, depth = attended.shape
    return pl.pallas_call(
        functools.partial(project_kernel, 0),
        out_shape=jax.ShapeDtypeStruct((rows, columns), BF16),
        grid=(columns // tile,),
        in_specs=[
            pl.BlockSpec((rows, depth), lambda i: (0, 0)),
            pl.BlockSpec((depth, tile), lambda i: (0, begin // tile + i)),
        ],
        out_specs=pl.BlockSpec((rows, tile), lambda i: (0, i)),
        compiler_params=pltpu.CompilerParams(vmem_limit_bytes=40 * 2**20),
    )(attended, weight)


def finish(operands, parts, gate_row, residual, begin, columns, tile, out):
    rows, width = residual.shape
    here = pl.BlockSpec((rows, tile), lambda i: (0, begin // tile + i))
    in_specs = []
    if operands:
        depth = operands[1].shape[0]
        in_specs += [pl.BlockSpec((rows, depth), lambda i: (0, 0))]
        in_specs += [pl.BlockSpec((depth, tile), lambda i: (0, begin // tile + i))]
    in_specs += [pl.BlockSpec((1, tile), lambda i: (0, begin // tile + i)), here]
    in_specs += [pl.BlockSpec((rows, tile), lambda i: (0, i))] * len(parts)
    arguments = [*operands, gate_row, residual, *parts]
    aliases = {}
    if out is not None:
        aliases = {len(arguments): 0}
        in_specs.append(pl.BlockSpec(memory_space=pl.ANY))
        arguments.append(out)
    kernel = project_kernel if operands else combine_kernel
    return pl.pallas_call(
        functools.partial(kernel, len(parts)),
        out_shape=jax.ShapeDtypeStruct((rows, width), BF16),
        grid=(columns // tile,),
        in_specs=in_specs,
        out_specs=here,
        input_output_aliases=aliases,
        compiler_params=pltpu.CompilerParams(vmem_limit_bytes=40 * 2**20),
    )(*arguments)


def move(block, n_span, sends, target):
    route = [(i, target(i)) for i in range(n_span) if sends(i) and 0 <= target(i) < n_span]
    return lax.ppermute(block, "span", route)


def on_device(
    queries,
    stacked_key_vectors,
    stacked_value_vectors,
    out_weight,
    residual,
    gate_table,
    noise_step,
    older_count,
):
    span_len = queries.shape[0]
    kv_heads = stacked_key_vectors.shape[1] // HEAD_SIZE
    group = queries.shape[1] // HEAD_SIZE // kv_heads
    model_width = out_weight.shape[1]
    n_span = lax.axis_size("span")
    n_head = lax.axis_size("head")
    my_span = lax.axis_index("span")
    my_head = lax.axis_index("head")
    rows = span_len // n_head

    own = jnp.stack([stacked_key_vectors, stacked_value_vectors])
    hop = functools.partial(move, n_span=n_span)
    places = [jnp.stack([(my_head + k) % n_head, my_span]).astype(jnp.int32) for k in range(n_head)]

    tile = model_width // 6
    chunks = [(0, 2), (2, 2), (4, 1), (5, 1)]
    first_columns = chunks[0][1] * tile

    def attend(k, blocks, state=None, last=False):
        weight = out_weight if last else None
        return attention(queries, places[k], older_count, rows, group, blocks, state, weight, first_columns)

    others = range(1, n_head)
    up = hop(own, sends=lambda i: True, target=lambda i: i + 4)
    across = hop(own, sends=lambda i: True, target=lambda i: i ^ 2)
    beside = hop(own, sends=lambda i: i & 1 == 0, target=lambda i: i ^ 1)
    states = [attend(k, {0: own}) for k in range(n_head)]
    up, across, beside, states = lax.optimization_barrier((up, across, beside, states))
    across_up = hop(across, sends=lambda i: i & 2 == 0, target=lambda i: i + 4)
    up_across = hop(up, sends=lambda i: i & 2 == 0, target=lambda i: i ^ 2)
    up_diagonal = hop(up, sends=lambda i: i & 2 > 0, target=lambda i: i + 2)
    up_seventh = hop(up, sends=lambda i: i & 1 > 0, target=lambda i: i + 3)
    across_beside = hop(across, sends=lambda i: i & 2 > 0, target=lambda i: i ^ 1)
    up_beside = hop(up, sends=lambda i: True, target=lambda i: i ^ 1)
    early = {1: beside, 2: across, 3: across_beside, 4: up, 5: up_beside}
    for k in others:
        states[k] = attend(k, early, states[k])
    across_up, up_across, up_diagonal, up_seventh, states = lax.optimization_barrier(
        (across_up, up_across, up_diagonal, up_seventh, states)
    )
    across_up_beside = hop(across_up, sends=lambda i: i & 2 == 0, target=lambda i: i ^ 1)
    up_across_beside = hop(up_across, sends=lambda i: i & 2 > 0, target=lambda i: i ^ 1)
    up_diagonal_beside = hop(up_diagonal, sends=lambda i: i & 2 == 0, target=lambda i: i ^ 1)
    late = {
        6: across_up,
        7: across_up_beside,
        8: up_across,
        9: up_across_beside,
        10: up_seventh,
        11: up_diagonal,
        12: up_diagonal_beside,
    }

    received = [[] for _ in chunks]
    for k in others:
        attended, partial = attend(k, late, states[k], last=True)
        route = [(i, (i + k) % n_head) for i in range(n_head)]
        received[0].append(lax.ppermute(partial, "head", route))
        for c, (begin, count) in list(enumerate(chunks))[1:]:
            partial = project(attended, out_weight, begin * tile, count * tile, tile)
            received[c].append(lax.ppermute(partial, "head", route))
            attended, partial = lax.optimization_barrier((attended, partial))

    states, attended = lax.optimization_barrier((states, attended))
    attended, kept = attend(0, {**early, **late}, states[0], last=True)
    gate_row = lax.dynamic_slice_in_dim(gate_table, noise_step[my_span], 1, 0)
    out = None
    for c, (begin, count) in enumerate(chunks):
        operands, parts = [], [kept, *received[c]]
        if c == len(chunks) - 1:
            parts = [project(attended, out_weight, begin * tile, count * tile, tile), *received[c]]
        elif c > 0:
            operands, parts = [attended, out_weight], received[c]
        out = finish(operands, parts, gate_row, residual, begin * tile, count * tile, tile, out)
    return out


def solution(mesh):
    in_specs = (
        P("span", "head"),
        P("span", "head"),
        P("span", "head"),
        P("head", None),
        P(("span", "head"), None),
        P(),
        P(),
        P(),
    )
    out_specs = P(("span", "head"), None)
    return jax.shard_map(
        on_device, mesh=mesh, in_specs=in_specs, out_specs=out_specs, check_vma=False
    )
```

```python
import functools
import math

import jax
import jax.numpy as jnp
from jax import lax
from jax.experimental import pallas as pl
from jax.experimental.pallas import tpu as pltpu
from jax.sharding import PartitionSpec as P

HEAD_SIZE = 128
MAX_BLOCKS = 8
EXPONENT_SCALE = math.log2(math.e) / math.sqrt(HEAD_SIZE)
TOTAL_LIMIT = 2.0**100
F32 = jnp.float32
BF16 = jnp.bfloat16


def slot_source(slot, my_span):
    core, y = my_span & 1, (my_span >> 1) & 1
    plane = my_span - 4
    return [
        (my_span, y >= 0),
        (my_span ^ 1, core == 1),
        (my_span ^ 2, y == 1),
        (my_span ^ 3, y == 1),
        (plane, y >= 0),
        (plane ^ 1, y >= 0),
        (plane ^ 2, y == 0),
        (plane ^ 3, y == 0),
        (plane ^ 2, y == 1),
        (plane ^ 3, y == 1),
        (my_span - 7, core == 0),
        (my_span - 6, y == 0),
        ((my_span - 6) ^ 1, y == 0),
    ][slot]


def attention_kernel(slots, rows, group, first, last, place, older_count, q_ref, *rest):
    kv_refs, rest = rest[: len(slots)], rest[len(slots) :]
    if not first:
        (sum_in, mark_in), rest = rest[:2], rest[2:]
    if last:
        weight_ref, out_ref, product_ref, keys, values, block_sems, scaled, acc, mark, attended, near_weight, arrived = rest
    else:
        sum_out, mark, keys, values, block_sems, scaled, acc = rest
    head = pl.program_id(0)
    n_head = pl.num_programs(0)
    now = lax.rem(head, 2)
    span = kv_refs[0].shape[1]
    all_rows = group * rows
    my_span = place[1]
    older_mine = older_count[my_span]

    places = []
    count = jnp.int32(0)
    for slot in slots:
        if slot == 0:
            seen = my_span >= 0
        else:
            source, used = slot_source(slot, my_span)
            seen = used & (source < my_span) & (my_span - source <= older_mine)
        places.append((seen, count))
        count = count + jnp.where(seen, 1, 0).astype(jnp.int32)

    def each_block(which, buffer, condition, act):
        columns = pl.ds(pl.multiple_of(which * HEAD_SIZE, HEAD_SIZE), HEAD_SIZE)
        left, right = pl.ds(0, HEAD_SIZE), pl.ds(HEAD_SIZE, HEAD_SIZE)
        for j, (seen, at) in enumerate(places):
            key_source = kv_refs[j].at[0, :, columns]
            copies = [(key_source, keys.at[buffer, at, :, left]), (key_source, keys.at[buffer, at, :, right])]
            for begin in range(0, span, HEAD_SIZE):
                part = pl.ds(begin, HEAD_SIZE)
                copies.append((kv_refs[j].at[1, part, columns], values.at[buffer, at, left, part]))
            copies = [
                pltpu.make_async_copy(source, target, block_sems.at[buffer, j, n])
                for n, (source, target) in enumerate(copies)
            ]

            @pl.when(seen & condition)
            def _():
                for copy in copies:
                    act(copy)

    each_block(head, now, head == 0, lambda copy: copy.start())
    each_block(head + 1, 1 - now, head + 1 < n_head, lambda copy: copy.start())
    if last:
        load = pltpu.make_async_copy(weight_ref.at[:, pl.ds(0, near_weight.shape[1])], near_weight, arrived)
        pl.when(head == 0)(load.start)

    @pl.when(head == 0)
    def _():
        values[:, :, HEAD_SIZE:, :] = jnp.ones(values.shape[:2] + (values.shape[2] - HEAD_SIZE, span), BF16)

    def scale():
        for h in range(group):
            q = q_ref[:, h * HEAD_SIZE : (h + 1) * HEAD_SIZE].astype(F32) * EXPONENT_SCALE
            q = q.T
            high = q.astype(BF16)
            scaled[:HEAD_SIZE, h * rows : (h + 1) * rows] = high
            scaled[HEAD_SIZE:, h * rows : (h + 1) * rows] = (q - high.astype(F32)).astype(BF16)

    def scores(block, at=slice(None)):
        return jnp.dot(keys[now, block], scaled[:, at], preferred_element_type=F32)

    def weigh(block, p):
        return jnp.dot(values[now, block], p.astype(BF16), preferred_element_type=F32)

    def add_block(block):
        acc[...] += weigh(block, jnp.exp2(scores(block) - mark[1:2, :]))

    if first:
        scale()
        each_block(head, now, head >= 0, lambda copy: copy.wait())
        s = scores(0)
        top = jnp.max(s, axis=0, keepdims=True)
        mark[0:1, :] = jnp.zeros((1, all_rows), F32)
        mark[1:2, :] = top
        acc[...] = weigh(0, jnp.exp2(s - top))
    else:
        pl.when(count > 0)(scale)
        acc[:HEAD_SIZE, :] = sum_in[...]
        acc[HEAD_SIZE:, :] = jnp.zeros((acc.shape[0] - HEAD_SIZE, all_rows), F32)
        mark[...] = mark_in[...]
        each_block(head, now, head >= 0, lambda copy: copy.wait())

    begin = 1 if first else 0
    if len(slots) > begin:
        pairs = (count - begin) // 2

        def two_blocks(i, carry):
            add_block(begin + 2 * i)
            add_block(begin + 2 * i + 1)
            return carry

        lax.fori_loop(0, pairs, two_blocks, 0)
        pl.when(begin + 2 * pairs < count)(functools.partial(add_block, count - 1))

        @pl.when(jnp.logical_not(jnp.max(acc[HEAD_SIZE : HEAD_SIZE + 8, :]) < TOTAL_LIMIT))
        def _():
            sub = math.gcd(all_rows, 384)

            def again(i, carry):
                at = pl.ds(pl.multiple_of(i * sub, sub), sub)
                acc[:, at] = jnp.zeros((acc.shape[0], sub), F32)
                if first:
                    mark[1:2, at] = jnp.full((1, sub), -1e30, F32)
                else:
                    acc[:HEAD_SIZE, at] = sum_in[:, at]
                    mark[:, at] = mark_in[:, at]

                def block_step(block, inner):
                    s = scores(block, at)
                    old_top = mark[1:2, at]
                    new_top = jnp.maximum(old_top, jnp.max(s, axis=0, keepdims=True))
                    shrink = jnp.exp2(old_top - new_top)
                    mark[0:1, at] = mark[0:1, at] * shrink
                    mark[1:2, at] = new_top
                    acc[:, at] = acc[:, at] * shrink + weigh(block, jnp.exp2(s - new_top))
                    return inner

                return lax.fori_loop(0, count, block_step, carry)

            lax.fori_loop(0, all_rows // sub, again, 0)

    total = mark[0:1, :] + acc[HEAD_SIZE : HEAD_SIZE + 1, :]
    if not last:
        mark[0:1, :] = total
        sum_out[...] = acc[:HEAD_SIZE, :]
        return
    for h in range(group):
        at = slice(h * rows, (h + 1) * rows)
        result = (acc[:HEAD_SIZE, at] / total[:, at]).T.astype(BF16)
        out_ref[:, h * HEAD_SIZE : (h + 1) * HEAD_SIZE] = result
        here = (head * group + h) * HEAD_SIZE
        attended[:, pl.ds(pl.multiple_of(here, HEAD_SIZE), HEAD_SIZE)] = result

    @pl.when(head == n_head - 1)
    def _():
        load.wait()
        tile = 512
        for begin in range(0, product_ref.shape[1], tile):
            at = slice(begin, begin + tile)
            product = jnp.dot(attended[...], near_weight[:, at], preferred_element_type=F32)
            product_ref[:, at] = product.astype(BF16)


def attention(queries, place, older_count, rows, group, blocks, state=None, weight=None, columns=0):
    slots = sorted(blocks)
    arrays = [blocks[slot] for slot in slots]
    first = state is None
    last = weight is not None
    kv_heads = arrays[0].shape[2] // HEAD_SIZE
    span = arrays[0].shape[1]
    width = group * HEAD_SIZE
    all_rows = group * rows
    n_block = min(MAX_BLOCKS, len(arrays))
    state_specs = [
        pl.BlockSpec((None, HEAD_SIZE, all_rows), lambda g, p, o: (g, 0, 0)),
        pl.BlockSpec((None, 8, all_rows), lambda g, p, o: (g, 0, 0)),
    ]
    high = HEAD_SIZE + 16
    in_specs = [pl.BlockSpec((rows, width), lambda g, p, o: (p[0], g))]
    in_specs += [pl.BlockSpec(memory_space=pltpu.HBM)] * len(arrays)
    scratch = [
        pltpu.VMEM((2, n_block, span, 2 * HEAD_SIZE), BF16),
        pltpu.VMEM((2, n_block, high, span), BF16),
        pltpu.SemaphoreType.DMA((2, len(arrays), 2 + span // HEAD_SIZE)),
        pltpu.VMEM((2 * HEAD_SIZE, all_rows), BF16),
        pltpu.VMEM((high, all_rows), F32),
    ]
    if not first:
        in_specs += state_specs
        arrays += list(state)
    if last:
        in_specs.append(pl.BlockSpec(memory_space=pltpu.HBM))
        arrays.append(weight)
        out_shape = [
            jax.ShapeDtypeStruct((rows, kv_heads * width), BF16),
            jax.ShapeDtypeStruct((rows, columns), BF16),
        ]
        out_specs = [
            pl.BlockSpec((rows, width), lambda g, p, o: (0, g)),
            pl.BlockSpec((rows, columns), lambda g, p, o: (0, 0)),
        ]
        scratch += [
            pltpu.VMEM((8, all_rows), F32),
            pltpu.VMEM((rows, kv_heads * width), BF16),
            pltpu.VMEM((weight.shape[0], columns), BF16),
            pltpu.SemaphoreType.DMA,
        ]
    else:
        out_shape = [pltpu.HBM((kv_heads, n, all_rows), F32) for n in (HEAD_SIZE, 8)]
        out_specs = state_specs
    return pl.pallas_call(
        functools.partial(attention_kernel, slots, rows, group, first, last),
        out_shape=out_shape,
        grid_spec=pltpu.PrefetchScalarGridSpec(
            num_scalar_prefetch=2,
            grid=(kv_heads,),
            in_specs=in_specs,
            out_specs=out_specs,
            scratch_shapes=scratch,
        ),
        compiler_params=pltpu.CompilerParams(vmem_limit_bytes=56 * 2**20),
    )(place, older_count, queries, *arrays)


def project_kernel(steps, a_ref, w_ref, *out_refs):
    step = pl.program_id(0)
    product = jnp.dot(a_ref[...], w_ref[...], preferred_element_type=F32).astype(BF16)
    for n, out_ref in enumerate(out_refs):

        @pl.when((step >= n * steps) & (step < (n + 1) * steps))
        def _(out_ref=out_ref):
            out_ref[...] = product


def project(attended, weight, begin, columns, n_out, tile):
    rows, depth = attended.shape
    steps = columns // tile
    return pl.pallas_call(
        functools.partial(project_kernel, steps),
        out_shape=[jax.ShapeDtypeStruct((rows, columns), BF16)] * n_out,
        grid=(n_out * steps,),
        in_specs=[
            pl.BlockSpec((rows, depth), lambda i: (0, 0)),
            pl.BlockSpec((depth, tile), lambda i: (0, begin // tile + i)),
        ],
        out_specs=[
            pl.BlockSpec((rows, tile), lambda i, n=n: (0, jnp.clip(i - n * steps, 0, steps - 1))) for n in range(n_out)
        ],
        compiler_params=pltpu.CompilerParams(vmem_limit_bytes=40 * 2**20),
    )(attended, weight)


def combine_kernel(n_part, place, noise_step, gate_ref, residual_ref, *rest):
    gate = gate_ref[pl.ds(noise_step[place[1]], 1), :]
    total = rest[0][...].astype(F32)
    for part in rest[1:n_part]:
        total = total + part[...].astype(F32)
    rest[-1][...] = (residual_ref[...].astype(F32) + gate * total).astype(BF16)


def combine(place, noise_step, gate_table, residual, kept, kept_begin, parts, begin, columns, tile, out):
    rows, width = residual.shape
    here = pl.BlockSpec((rows, tile), lambda i, p, n: (0, begin // tile + i))
    in_specs = [pl.BlockSpec((gate_table.shape[0], tile), lambda i, p, n: (0, begin // tile + i)), here]
    in_specs += [pl.BlockSpec((rows, tile), lambda i, p, n: (0, kept_begin // tile + i))]
    in_specs += [pl.BlockSpec((rows, tile), lambda i, p, n: (0, i))] * len(parts)
    arguments = [place, noise_step, gate_table, residual, kept, *parts]
    aliases = {}
    if out is not None:
        aliases = {len(arguments): 0}
        in_specs.append(pl.BlockSpec(memory_space=pl.ANY))
        arguments.append(out)
    return pl.pallas_call(
        functools.partial(combine_kernel, 1 + len(parts)),
        out_shape=jax.ShapeDtypeStruct((rows, width), BF16),
        grid_spec=pltpu.PrefetchScalarGridSpec(
            num_scalar_prefetch=2, grid=(columns // tile,), in_specs=in_specs, out_specs=here
        ),
        input_output_aliases=aliases,
        compiler_params=pltpu.CompilerParams(vmem_limit_bytes=40 * 2**20),
    )(*arguments)


def move(block, n_span, sends, target):
    route = [(i, target(i)) for i in range(n_span) if sends(i) and 0 <= target(i) < n_span]
    return lax.ppermute(block, "span", route)


def on_device(
    queries,
    stacked_key_vectors,
    stacked_value_vectors,
    out_weight,
    residual,
    gate_table,
    noise_step,
    older_count,
):
    span_len = queries.shape[0]
    kv_heads = stacked_key_vectors.shape[1] // HEAD_SIZE
    group = queries.shape[1] // HEAD_SIZE // kv_heads
    model_width = out_weight.shape[1]
    n_span = lax.axis_size("span")
    n_head = lax.axis_size("head")
    my_span = lax.axis_index("span")
    my_head = lax.axis_index("head")
    rows = span_len // n_head

    tiles = stacked_value_vectors.reshape(span_len // HEAD_SIZE, HEAD_SIZE, kv_heads, HEAD_SIZE)
    own = jnp.stack([stacked_key_vectors, tiles.transpose(0, 3, 2, 1).reshape(stacked_value_vectors.shape)])
    hop = functools.partial(move, n_span=n_span)
    places = [jnp.stack([(my_head + k) % n_head, my_span]).astype(jnp.int32) for k in range(n_head)]

    tile = model_width // 6
    chunk = 2 * tile

    def attend(k, blocks, state=None, columns=0):
        weight = out_weight if columns else None
        return attention(queries, places[k], older_count, rows, group, blocks, state, weight, columns)

    others = range(1, n_head)
    up = hop(own, sends=lambda i: True, target=lambda i: i + 4)
    across = hop(own, sends=lambda i: True, target=lambda i: i ^ 2)
    beside = hop(own, sends=lambda i: i & 1 == 0, target=lambda i: i ^ 1)
    states = [attend(k, {0: own}) for k in range(n_head)]
    up, across, beside, states = lax.optimization_barrier((up, across, beside, states))
    across_up = hop(across, sends=lambda i: i & 2 == 0, target=lambda i: i + 4)
    up_across = hop(up, sends=lambda i: i & 2 == 0, target=lambda i: i ^ 2)
    up_diagonal = hop(up, sends=lambda i: i & 2 > 0, target=lambda i: i + 2)
    up_seventh = hop(up, sends=lambda i: i & 1 > 0, target=lambda i: i + 3)
    across_beside = hop(across, sends=lambda i: i & 2 > 0, target=lambda i: i ^ 1)
    up_beside = hop(up, sends=lambda i: True, target=lambda i: i ^ 1)
    early = {1: beside, 2: across, 3: across_beside, 4: up, 5: up_beside}
    for k in others:
        states[k] = attend(k, early, states[k])
    across_up, up_across, up_diagonal, up_seventh, states = lax.optimization_barrier(
        (across_up, up_across, up_diagonal, up_seventh, states)
    )
    across_up_beside = hop(across_up, sends=lambda i: i & 2 == 0, target=lambda i: i ^ 1)
    up_across_beside = hop(up_across, sends=lambda i: i & 2 > 0, target=lambda i: i ^ 1)
    up_diagonal_beside = hop(up_diagonal, sends=lambda i: i & 2 == 0, target=lambda i: i ^ 1)
    late = {
        6: across_up,
        7: across_up_beside,
        8: up_across,
        9: up_across_beside,
        10: up_seventh,
        11: up_diagonal,
        12: up_diagonal_beside,
    }

    received = []
    for k in others:
        attended, partial = attend(k, late, states[k], chunk)
        route = [(i, (i + k) % n_head) for i in range(n_head)]
        begun = lax.ppermute(partial, "head", route)
        partials = project(attended, out_weight, chunk, chunk, 2, tile)
        received.append([begun] + [lax.ppermute(partial, "head", route) for partial in partials])

    states, attended = lax.optimization_barrier((states, attended))
    attended, kept = attend(0, {**early, **late}, states[0], 2 * chunk)
    (kept_end,) = project(attended, out_weight, 2 * chunk, chunk, 1, tile)
    out = None
    for c in range(3):
        parts = [got[c] for got in received]
        at = (kept, c * chunk) if c < 2 else (kept_end, 0)
        out = combine(places[0], noise_step, gate_table, residual, *at, parts, c * chunk, chunk, tile, out)
    return out


def solution(mesh):
    in_specs = (
        P("span", "head"),
        P("span", "head"),
        P("span", "head"),
        P("head", None),
        P(("span", "head"), None),
        P(),
        P(),
        P(),
    )
    out_specs = P(("span", "head"), None)
    return jax.shard_map(
        on_device, mesh=mesh, in_specs=in_specs, out_specs=out_specs, check_vma=False
    )
```

```python
import functools
import math

import jax
import jax.numpy as jnp
from jax import lax
from jax.experimental import pallas as pl
from jax.experimental.pallas import tpu as pltpu
from jax.sharding import PartitionSpec as P

HEAD_SIZE = 128
MAX_BLOCKS = 8
EXPONENT_SCALE = math.log2(math.e) / math.sqrt(HEAD_SIZE)
TOTAL_LIMIT = 2.0**100
EARLY = (1, 2, 3, 4, 5)
EARLY_LIMIT = 5
F32 = jnp.float32
BF16 = jnp.bfloat16


def slot_source(slot, my_span):
    core, y = my_span & 1, (my_span >> 1) & 1
    plane = my_span - 4
    return [
        (my_span, y >= 0),
        (my_span ^ 1, core == 1),
        (my_span ^ 2, y == 1),
        (my_span ^ 3, y == 1),
        (plane, y >= 0),
        (plane ^ 1, y >= 0),
        (plane ^ 2, y == 0),
        (plane ^ 3, y == 0),
        (plane ^ 2, y == 1),
        (plane ^ 3, y == 1),
        (my_span - 7, core == 0),
        (my_span - 6, y == 0),
        ((my_span - 6) ^ 1, y == 0),
    ][slot]


def attention_kernel(slots, rows, group, first, last, share, place, older_count, q_ref, *rest):
    kv_refs, rest = rest[: len(slots)], rest[len(slots) :]
    if not first:
        (sum_in, mark_in), rest = rest[:2], rest[2:]
    if last:
        weight_ref, out_ref, product_ref, keys, values, block_sems, scaled, acc, mark, attended, near_weight, arrived = rest
    else:
        sum_out, mark, keys, values, block_sems, scaled, acc = rest
    head = pl.program_id(0)
    n_head = pl.num_programs(0)
    now = lax.rem(head, 2)
    span = kv_refs[0].shape[1]
    all_rows = group * rows
    my_span = place[1]
    older_mine = older_count[my_span]

    def in_view(slot):
        source, used = slot_source(slot, my_span)
        return used & (source <= my_span) & (my_span - source <= older_mine)

    def number(flags):
        return sum(jnp.where(flag, 1, 0).astype(jnp.int32) for flag in flags)

    views = [in_view(slot) for slot in slots]
    if share:
        earlies = [in_view(slot) for slot in EARLY]
        n_early = number(earlies)
        first_part = jnp.maximum(EARLY_LIMIT - n_early, 0)
        for n, slot in enumerate(EARLY):
            before = number(earlies[:n]) if n else 0
            taken = before < first_part
            views[slots.index(slot)] = earlies[n] & (taken if share == "begin" else jnp.logical_not(taken))
    places = []
    count = jnp.int32(0)
    for seen in views:
        places.append((seen, count))
        count = count + jnp.where(seen, 1, 0).astype(jnp.int32)

    def each_block(which, buffer, condition, act):
        columns = pl.ds(pl.multiple_of(which * HEAD_SIZE, HEAD_SIZE), HEAD_SIZE)
        left, right = pl.ds(0, HEAD_SIZE), pl.ds(HEAD_SIZE, HEAD_SIZE)
        for j, (seen, at) in enumerate(places):
            key_source = kv_refs[j].at[0, :, columns]
            copies = [(key_source, keys.at[buffer, at, :, left]), (key_source, keys.at[buffer, at, :, right])]
            for begin in range(0, span, HEAD_SIZE):
                part = pl.ds(begin, HEAD_SIZE)
                copies.append((kv_refs[j].at[1, part, columns], values.at[buffer, at, left, part]))
            copies = [
                pltpu.make_async_copy(source, target, block_sems.at[buffer, j, n])
                for n, (source, target) in enumerate(copies)
            ]

            @pl.when(seen & condition)
            def _():
                for copy in copies:
                    act(copy)

    each_block(head, now, head == 0, lambda copy: copy.start())
    each_block(head + 1, 1 - now, head + 1 < n_head, lambda copy: copy.start())
    if last:
        load = pltpu.make_async_copy(weight_ref.at[:, pl.ds(0, near_weight.shape[1])], near_weight, arrived)
        pl.when(head == 0)(load.start)

    @pl.when(head == 0)
    def _():
        values[:, :, HEAD_SIZE:, :] = jnp.ones(values.shape[:2] + (values.shape[2] - HEAD_SIZE, span), BF16)

    def scale():
        for h in range(group):
            q = q_ref[:, h * HEAD_SIZE : (h + 1) * HEAD_SIZE].astype(F32) * EXPONENT_SCALE
            q = q.T
            high = q.astype(BF16)
            scaled[:HEAD_SIZE, h * rows : (h + 1) * rows] = high
            scaled[HEAD_SIZE:, h * rows : (h + 1) * rows] = (q - high.astype(F32)).astype(BF16)

    def scores(block, at=slice(None)):
        return jnp.dot(keys[now, block], scaled[:, at], preferred_element_type=F32)

    def weigh(block, p):
        return jnp.dot(values[now, block], p.astype(BF16), preferred_element_type=F32)

    def add_block(block):
        acc[...] += weigh(block, jnp.exp2(scores(block) - mark[1:2, :]))

    if first:
        scale()
        each_block(head, now, head >= 0, lambda copy: copy.wait())
        s = scores(0)
        top = jnp.max(s, axis=0, keepdims=True)
        mark[0:1, :] = jnp.zeros((1, all_rows), F32)
        mark[1:2, :] = top
        acc[...] = weigh(0, jnp.exp2(s - top))
    else:
        pl.when(count > 0)(scale)
        acc[:HEAD_SIZE, :] = sum_in[...]
        acc[HEAD_SIZE:, :] = jnp.zeros((acc.shape[0] - HEAD_SIZE, all_rows), F32)
        mark[...] = mark_in[...]
        each_block(head, now, head >= 0, lambda copy: copy.wait())

    begin = 1 if first else 0
    if len(slots) > begin:
        pairs = (count - begin) // 2

        def two_blocks(i, carry):
            add_block(begin + 2 * i)
            add_block(begin + 2 * i + 1)
            return carry

        lax.fori_loop(0, pairs, two_blocks, 0)
        pl.when(begin + 2 * pairs < count)(functools.partial(add_block, count - 1))

        @pl.when(jnp.logical_not(jnp.max(acc[HEAD_SIZE : HEAD_SIZE + 8, :]) < TOTAL_LIMIT))
        def _():
            sub = math.gcd(all_rows, 384)

            def again(i, carry):
                at = pl.ds(pl.multiple_of(i * sub, sub), sub)
                acc[:, at] = jnp.zeros((acc.shape[0], sub), F32)
                if first:
                    mark[1:2, at] = jnp.full((1, sub), -1e30, F32)
                else:
                    acc[:HEAD_SIZE, at] = sum_in[:, at]
                    mark[:, at] = mark_in[:, at]

                def block_step(block, inner):
                    s = scores(block, at)
                    old_top = mark[1:2, at]
                    new_top = jnp.maximum(old_top, jnp.max(s, axis=0, keepdims=True))
                    shrink = jnp.exp2(old_top - new_top)
                    mark[0:1, at] = mark[0:1, at] * shrink
                    mark[1:2, at] = new_top
                    acc[:, at] = acc[:, at] * shrink + weigh(block, jnp.exp2(s - new_top))
                    return inner

                return lax.fori_loop(0, count, block_step, carry)

            lax.fori_loop(0, all_rows // sub, again, 0)

    total = mark[0:1, :] + acc[HEAD_SIZE : HEAD_SIZE + 1, :]
    if not last:
        mark[0:1, :] = total
        sum_out[...] = acc[:HEAD_SIZE, :]
        return
    for h in range(group):
        at = slice(h * rows, (h + 1) * rows)
        result = (acc[:HEAD_SIZE, at] / total[:, at]).T.astype(BF16)
        out_ref[:, h * HEAD_SIZE : (h + 1) * HEAD_SIZE] = result
        here = (head * group + h) * HEAD_SIZE
        attended[:, pl.ds(pl.multiple_of(here, HEAD_SIZE), HEAD_SIZE)] = result

    @pl.when(head == n_head - 1)
    def _():
        load.wait()
        tile = 512
        for begin in range(0, product_ref.shape[1], tile):
            at = slice(begin, begin + tile)
            product = jnp.dot(attended[...], near_weight[:, at], preferred_element_type=F32)
            product_ref[:, at] = product.astype(BF16)


def attention(queries, place, older_count, rows, group, blocks, state=None, weight=None, columns=0, share=""):
    slots = sorted(blocks)
    arrays = [blocks[slot] for slot in slots]
    first = state is None
    last = weight is not None
    kv_heads = arrays[0].shape[2] // HEAD_SIZE
    span = arrays[0].shape[1]
    width = group * HEAD_SIZE
    all_rows = group * rows
    n_block = min(MAX_BLOCKS, len(arrays))
    state_specs = [
        pl.BlockSpec((None, HEAD_SIZE, all_rows), lambda g, p, o: (g, 0, 0)),
        pl.BlockSpec((None, 8, all_rows), lambda g, p, o: (g, 0, 0)),
    ]
    high = HEAD_SIZE + 16
    in_specs = [pl.BlockSpec((rows, width), lambda g, p, o: (p[0], g))]
    in_specs += [pl.BlockSpec(memory_space=pl.ANY)] * len(arrays)
    scratch = [
        pltpu.VMEM((2, n_block, span, 2 * HEAD_SIZE), BF16),
        pltpu.VMEM((2, n_block, high, span), BF16),
        pltpu.SemaphoreType.DMA((2, len(arrays), 2 + span // HEAD_SIZE)),
        pltpu.VMEM((2 * HEAD_SIZE, all_rows), BF16),
        pltpu.VMEM((high, all_rows), F32),
    ]
    if not first:
        in_specs += state_specs
        arrays += list(state)
    if last:
        in_specs.append(pl.BlockSpec(memory_space=pl.ANY))
        arrays.append(weight)
        out_shape = [
            pltpu.HBM((rows, kv_heads * width), BF16),
            pltpu.HBM((rows, columns), BF16),
        ]
        out_specs = [
            pl.BlockSpec((rows, width), lambda g, p, o: (0, g)),
            pl.BlockSpec((rows, columns), lambda g, p, o: (0, 0)),
        ]
        scratch += [
            pltpu.VMEM((8, all_rows), F32),
            pltpu.VMEM((rows, kv_heads * width), BF16),
            pltpu.VMEM((weight.shape[0], columns), BF16),
            pltpu.SemaphoreType.DMA,
        ]
    else:
        out_shape = [pltpu.HBM((kv_heads, n, all_rows), F32) for n in (HEAD_SIZE, 8)]
        out_specs = state_specs
    return pl.pallas_call(
        functools.partial(attention_kernel, slots, rows, group, first, last, share),
        out_shape=out_shape,
        grid_spec=pltpu.PrefetchScalarGridSpec(
            num_scalar_prefetch=2,
            grid=(kv_heads,),
            in_specs=in_specs,
            out_specs=out_specs,
            scratch_shapes=scratch,
        ),
        compiler_params=pltpu.CompilerParams(vmem_limit_bytes=56 * 2**20),
    )(place, older_count, queries, *arrays)


def project_kernel(steps, a_ref, w_ref, *out_refs):
    step = pl.program_id(0)
    product = jnp.dot(a_ref[...], w_ref[...], preferred_element_type=F32).astype(BF16)
    for n, out_ref in enumerate(out_refs):

        @pl.when((step >= n * steps) & (step < (n + 1) * steps))
        def _(out_ref=out_ref):
            out_ref[...] = product


def project(attended, weight, begin, columns, n_out, tile):
    rows, depth = attended.shape
    steps = columns // tile
    return pl.pallas_call(
        functools.partial(project_kernel, steps),
        out_shape=[jax.ShapeDtypeStruct((rows, columns), BF16)] * n_out,
        grid=(n_out * steps,),
        in_specs=[
            pl.BlockSpec((rows, depth), lambda i: (0, 0)),
            pl.BlockSpec((depth, tile), lambda i: (0, begin // tile + i)),
        ],
        out_specs=[
            pl.BlockSpec((rows, tile), lambda i, n=n: (0, jnp.clip(i - n * steps, 0, steps - 1))) for n in range(n_out)
        ],
        compiler_params=pltpu.CompilerParams(vmem_limit_bytes=40 * 2**20),
    )(attended, weight)


def combine_kernel(n_part, place, noise_step, gate_ref, residual_ref, *rest):
    gate = gate_ref[pl.ds(noise_step[place[1]], 1), :]
    total = rest[0][...].astype(F32)
    for part in rest[1:n_part]:
        total = total + part[...].astype(F32)
    rest[-1][...] = (residual_ref[...].astype(F32) + gate * total).astype(BF16)


def combine(place, noise_step, gate_table, residual, kept, kept_begin, parts, begin, columns, tile, out):
    rows, width = residual.shape
    here = pl.BlockSpec((rows, tile), lambda i, p, n: (0, begin // tile + i))
    in_specs = [pl.BlockSpec((gate_table.shape[0], tile), lambda i, p, n: (0, begin // tile + i)), here]
    in_specs += [pl.BlockSpec((rows, tile), lambda i, p, n: (0, kept_begin // tile + i))]
    in_specs += [pl.BlockSpec((rows, tile), lambda i, p, n: (0, i))] * len(parts)
    arguments = [place, noise_step, gate_table, residual, kept, *parts]
    aliases = {}
    if out is not None:
        aliases = {len(arguments): 0}
        in_specs.append(pl.BlockSpec(memory_space=pl.ANY))
        arguments.append(out)
    return pl.pallas_call(
        functools.partial(combine_kernel, 1 + len(parts)),
        out_shape=jax.ShapeDtypeStruct((rows, width), BF16),
        grid_spec=pltpu.PrefetchScalarGridSpec(
            num_scalar_prefetch=2, grid=(columns // tile,), in_specs=in_specs, out_specs=here
        ),
        input_output_aliases=aliases,
        compiler_params=pltpu.CompilerParams(vmem_limit_bytes=40 * 2**20),
    )(*arguments)


def move(block, n_span, sends, target):
    route = [(i, target(i)) for i in range(n_span) if sends(i) and 0 <= target(i) < n_span]
    return lax.ppermute(block, "span", route)


def on_device(
    queries,
    stacked_key_vectors,
    stacked_value_vectors,
    out_weight,
    residual,
    gate_table,
    noise_step,
    older_count,
):
    span_len = queries.shape[0]
    kv_heads = stacked_key_vectors.shape[1] // HEAD_SIZE
    group = queries.shape[1] // HEAD_SIZE // kv_heads
    model_width = out_weight.shape[1]
    n_span = lax.axis_size("span")
    n_head = lax.axis_size("head")
    my_span = lax.axis_index("span")
    my_head = lax.axis_index("head")
    rows = span_len // n_head

    tiles = stacked_value_vectors.reshape(span_len // HEAD_SIZE, HEAD_SIZE, kv_heads, HEAD_SIZE)
    own = jnp.stack([stacked_key_vectors, tiles.transpose(0, 3, 2, 1).reshape(stacked_value_vectors.shape)])
    hop = functools.partial(move, n_span=n_span)
    places = [jnp.stack([(my_head + k) % n_head, my_span]).astype(jnp.int32) for k in range(n_head)]

    tile = model_width // 6
    chunk = 2 * tile

    def attend(k, blocks, state=None, columns=0, share=""):
        weight = out_weight if columns else None
        return attention(queries, places[k], older_count, rows, group, blocks, state, weight, columns, share)

    others = range(1, n_head)
    up = hop(own, sends=lambda i: True, target=lambda i: i + 4)
    across = hop(own, sends=lambda i: True, target=lambda i: i ^ 2)
    beside = hop(own, sends=lambda i: i & 1 == 0, target=lambda i: i ^ 1)
    states = [attend(k, {0: own}) for k in range(n_head)]
    up, across, beside, states = lax.optimization_barrier((up, across, beside, states))
    across_up = hop(across, sends=lambda i: i & 2 == 0, target=lambda i: i + 4)
    up_across = hop(up, sends=lambda i: i & 2 == 0, target=lambda i: i ^ 2)
    up_diagonal = hop(up, sends=lambda i: i & 2 > 0, target=lambda i: i + 2)
    up_seventh = hop(up, sends=lambda i: i & 1 > 0, target=lambda i: i + 3)
    across_beside = hop(across, sends=lambda i: i & 2 > 0, target=lambda i: i ^ 1)
    up_beside = hop(up, sends=lambda i: True, target=lambda i: i ^ 1)
    early = {1: beside, 2: across, 3: across_beside, 4: up, 5: up_beside}
    for k in others:
        states[k] = attend(k, early, states[k])
    states[0] = attend(0, early, states[0], share="begin")
    across_up, up_across, up_diagonal, up_seventh, states = lax.optimization_barrier(
        (across_up, up_across, up_diagonal, up_seventh, states)
    )
    across_up_beside = hop(across_up, sends=lambda i: i & 2 == 0, target=lambda i: i ^ 1)
    up_across_beside = hop(up_across, sends=lambda i: i & 2 > 0, target=lambda i: i ^ 1)
    up_diagonal_beside = hop(up_diagonal, sends=lambda i: i & 2 == 0, target=lambda i: i ^ 1)
    late = {
        6: across_up,
        7: across_up_beside,
        8: up_across,
        9: up_across_beside,
        10: up_seventh,
        11: up_diagonal,
        12: up_diagonal_beside,
    }

    received = []
    for k in others:
        attended, partial = attend(k, late, states[k], chunk)
        route = [(i, (i + k) % n_head) for i in range(n_head)]
        begun = lax.ppermute(partial, "head", route)
        partials = project(attended, out_weight, chunk, chunk, 2, tile)
        received.append([begun] + [lax.ppermute(partial, "head", route) for partial in partials])

    states, attended = lax.optimization_barrier((states, attended))
    attended, kept = attend(0, {**early, **late}, states[0], 2 * chunk, share="end")
    (kept_end,) = project(attended, out_weight, 2 * chunk, chunk, 1, tile)
    out = None
    for c in range(3):
        parts = [got[c] for got in received]
        at = (kept, c * chunk) if c < 2 else (kept_end, 0)
        out = combine(places[0], noise_step, gate_table, residual, *at, parts, c * chunk, chunk, tile, out)
    return out


def solution(mesh):
    in_specs = (
        P("span", "head"),
        P("span", "head"),
        P("span", "head"),
        P("head", None),
        P(("span", "head"), None),
        P(),
        P(),
        P(),
    )
    out_specs = P(("span", "head"), None)
    return jax.shard_map(
        on_device, mesh=mesh, in_specs=in_specs, out_specs=out_specs, check_vma=False
    )
```

```python
import functools
import math

import jax
import jax.numpy as jnp
from jax import lax
from jax.experimental import pallas as pl
from jax.experimental.pallas import tpu as pltpu
from jax.sharding import PartitionSpec as P

HEAD_SIZE = 128
MAX_BLOCKS = 8
EXPONENT_SCALE = math.log2(math.e) / math.sqrt(HEAD_SIZE)
TOTAL_LIMIT = 2.0**100
EARLY = (1, 2, 3, 4, 5)
EARLY_LIMIT = 5
F32 = jnp.float32
BF16 = jnp.bfloat16


def slot_source(slot, my_span):
    core, y = my_span & 1, (my_span >> 1) & 1
    plane = my_span - 4
    return [
        (my_span, y >= 0),
        (my_span ^ 1, core == 1),
        (my_span ^ 2, y == 1),
        (my_span ^ 3, y == 1),
        (plane, y >= 0),
        (plane ^ 1, y >= 0),
        (plane ^ 2, y == 0),
        (plane ^ 3, y == 0),
        (plane ^ 2, y == 1),
        (plane ^ 3, y == 1),
        (my_span - 7, core == 0),
        (my_span - 6, y == 0),
        ((my_span - 6) ^ 1, y == 0),
    ][slot]


def attention_kernel(slots, rows, group, first, last, share, place, older_count, q_ref, *rest):
    kv_refs, rest = rest[: len(slots)], rest[len(slots) :]
    if not first:
        (sum_in, mark_in), rest = rest[:2], rest[2:]
    if last:
        weight_ref, out_ref, product_ref, keys, values, block_sems, scaled, acc, mark, attended, near_weight, arrived = rest
    else:
        sum_out, mark, keys, values, block_sems, scaled, acc = rest
    head = pl.program_id(0)
    n_head = pl.num_programs(0)
    now = lax.rem(head, 2)
    span = kv_refs[0].shape[1]
    all_rows = group * rows
    my_span = place[1]
    older_mine = older_count[my_span]

    def in_view(slot):
        source, used = slot_source(slot, my_span)
        return used & (source <= my_span) & (my_span - source <= older_mine)

    def number(flags):
        return sum(jnp.where(flag, 1, 0).astype(jnp.int32) for flag in flags)

    views = [in_view(slot) for slot in slots]
    if share:
        earlies = [in_view(slot) for slot in EARLY]
        n_early = number(earlies)
        first_part = jnp.maximum(EARLY_LIMIT - n_early, 0)
        for n, slot in enumerate(EARLY):
            before = number(earlies[:n]) if n else 0
            taken = before < first_part
            views[slots.index(slot)] = earlies[n] & (taken if share == "begin" else jnp.logical_not(taken))
    places = []
    count = jnp.int32(0)
    for seen in views:
        places.append((seen, count))
        count = count + jnp.where(seen, 1, 0).astype(jnp.int32)

    def each_block(which, buffer, condition, act):
        columns = pl.ds(pl.multiple_of(which * HEAD_SIZE, HEAD_SIZE), HEAD_SIZE)
        left, right = pl.ds(0, HEAD_SIZE), pl.ds(HEAD_SIZE, HEAD_SIZE)
        for j, (seen, at) in enumerate(places):
            key_source = kv_refs[j].at[0, :, columns]
            copies = [(key_source, keys.at[buffer, at, :, left]), (key_source, keys.at[buffer, at, :, right])]
            for begin in range(0, span, HEAD_SIZE):
                part = pl.ds(begin, HEAD_SIZE)
                copies.append((kv_refs[j].at[1, part, columns], values.at[buffer, at, left, part]))
            copies = [
                pltpu.make_async_copy(source, target, block_sems.at[buffer, j, n])
                for n, (source, target) in enumerate(copies)
            ]

            @pl.when(seen & condition)
            def _():
                for copy in copies:
                    act(copy)

    each_block(head, now, head == 0, lambda copy: copy.start())
    each_block(head + 1, 1 - now, head + 1 < n_head, lambda copy: copy.start())
    if last:
        load = pltpu.make_async_copy(weight_ref.at[:, pl.ds(0, near_weight.shape[1])], near_weight, arrived)
        pl.when(head == 0)(load.start)

    @pl.when(head == 0)
    def _():
        values[:, :, HEAD_SIZE:, :] = jnp.ones(values.shape[:2] + (values.shape[2] - HEAD_SIZE, span), BF16)

    def scale():
        for h in range(group):
            q = q_ref[:, h * HEAD_SIZE : (h + 1) * HEAD_SIZE].astype(F32) * EXPONENT_SCALE
            q = q.T
            high = q.astype(BF16)
            scaled[:HEAD_SIZE, h * rows : (h + 1) * rows] = high
            scaled[HEAD_SIZE:, h * rows : (h + 1) * rows] = (q - high.astype(F32)).astype(BF16)

    def scores(block, at=slice(None)):
        return jnp.dot(keys[now, block], scaled[:, at], preferred_element_type=F32)

    def weigh(block, p):
        return jnp.dot(values[now, block], p.astype(BF16), preferred_element_type=F32)

    def add_block(block):
        acc[...] += weigh(block, jnp.exp2(scores(block) - mark[1:2, :]))

    if first:
        scale()
        each_block(head, now, head >= 0, lambda copy: copy.wait())
        s = scores(0)
        top = jnp.max(s, axis=0, keepdims=True)
        mark[0:1, :] = jnp.zeros((1, all_rows), F32)
        mark[1:2, :] = top
        acc[...] = weigh(0, jnp.exp2(s - top))
    else:
        pl.when(count > 0)(scale)
        acc[:HEAD_SIZE, :] = sum_in[...]
        acc[HEAD_SIZE:, :] = jnp.zeros((acc.shape[0] - HEAD_SIZE, all_rows), F32)
        mark[...] = mark_in[...]
        each_block(head, now, head >= 0, lambda copy: copy.wait())

    begin = 1 if first else 0
    if len(slots) > begin:
        pairs = (count - begin) // 2

        def two_blocks(i, carry):
            add_block(begin + 2 * i)
            add_block(begin + 2 * i + 1)
            return carry

        lax.fori_loop(0, pairs, two_blocks, 0)
        pl.when(begin + 2 * pairs < count)(functools.partial(add_block, count - 1))

        @pl.when(jnp.logical_not(jnp.max(acc[HEAD_SIZE : HEAD_SIZE + 8, :]) < TOTAL_LIMIT))
        def _():
            sub = math.gcd(all_rows, 384)

            def again(i, carry):
                at = pl.ds(pl.multiple_of(i * sub, sub), sub)
                acc[:, at] = jnp.zeros((acc.shape[0], sub), F32)
                if first:
                    mark[1:2, at] = jnp.full((1, sub), -1e30, F32)
                else:
                    acc[:HEAD_SIZE, at] = sum_in[:, at]
                    mark[:, at] = mark_in[:, at]

                def block_step(block, inner):
                    s = scores(block, at)
                    old_top = mark[1:2, at]
                    new_top = jnp.maximum(old_top, jnp.max(s, axis=0, keepdims=True))
                    shrink = jnp.exp2(old_top - new_top)
                    mark[0:1, at] = mark[0:1, at] * shrink
                    mark[1:2, at] = new_top
                    acc[:, at] = acc[:, at] * shrink + weigh(block, jnp.exp2(s - new_top))
                    return inner

                return lax.fori_loop(0, count, block_step, carry)

            lax.fori_loop(0, all_rows // sub, again, 0)

    total = mark[0:1, :] + acc[HEAD_SIZE : HEAD_SIZE + 1, :]
    if not last:
        mark[0:1, :] = total
        sum_out[...] = acc[:HEAD_SIZE, :]
        return
    for h in range(group):
        at = slice(h * rows, (h + 1) * rows)
        result = (acc[:HEAD_SIZE, at] / total[:, at]).T.astype(BF16)
        out_ref[:, h * HEAD_SIZE : (h + 1) * HEAD_SIZE] = result
        here = (head * group + h) * HEAD_SIZE
        attended[:, pl.ds(pl.multiple_of(here, HEAD_SIZE), HEAD_SIZE)] = result

    @pl.when(head == n_head - 1)
    def _():
        load.wait()
        tile = 512
        for begin in range(0, product_ref.shape[1], tile):
            at = slice(begin, begin + tile)
            product = jnp.dot(attended[...], near_weight[:, at], preferred_element_type=F32)
            product_ref[:, at] = product.astype(BF16)


def attention(queries, place, older_count, rows, group, blocks, state=None, weight=None, columns=0, share=""):
    slots = sorted(blocks)
    arrays = [blocks[slot] for slot in slots]
    first = state is None
    last = weight is not None
    kv_heads = arrays[0].shape[2] // HEAD_SIZE
    span = arrays[0].shape[1]
    width = group * HEAD_SIZE
    all_rows = group * rows
    n_block = min(MAX_BLOCKS, len(arrays))
    state_specs = [
        pl.BlockSpec((None, HEAD_SIZE, all_rows), lambda g, p, o: (g, 0, 0)),
        pl.BlockSpec((None, 8, all_rows), lambda g, p, o: (g, 0, 0)),
    ]
    high = HEAD_SIZE + 16
    in_specs = [pl.BlockSpec((rows, width), lambda g, p, o: (p[0], g))]
    in_specs += [pl.BlockSpec(memory_space=pl.ANY)] * len(arrays)
    scratch = [
        pltpu.VMEM((2, n_block, span, 2 * HEAD_SIZE), BF16),
        pltpu.VMEM((2, n_block, high, span), BF16),
        pltpu.SemaphoreType.DMA((2, len(arrays), 2 + span // HEAD_SIZE)),
        pltpu.VMEM((2 * HEAD_SIZE, all_rows), BF16),
        pltpu.VMEM((high, all_rows), F32),
    ]
    if not first:
        in_specs += state_specs
        arrays += list(state)
    if last:
        in_specs.append(pl.BlockSpec(memory_space=pl.ANY))
        arrays.append(weight)
        out_shape = [
            pltpu.HBM((rows, kv_heads * width), BF16),
            pltpu.HBM((rows, columns), BF16),
        ]
        out_specs = [
            pl.BlockSpec((rows, width), lambda g, p, o: (0, g)),
            pl.BlockSpec((rows, columns), lambda g, p, o: (0, 0)),
        ]
        scratch += [
            pltpu.VMEM((8, all_rows), F32),
            pltpu.VMEM((rows, kv_heads * width), BF16),
            pltpu.VMEM((weight.shape[0], columns), BF16),
            pltpu.SemaphoreType.DMA,
        ]
    else:
        out_shape = [pltpu.HBM((kv_heads, n, all_rows), F32) for n in (HEAD_SIZE, 8)]
        out_specs = state_specs
    return pl.pallas_call(
        functools.partial(attention_kernel, slots, rows, group, first, last, share),
        out_shape=out_shape,
        grid_spec=pltpu.PrefetchScalarGridSpec(
            num_scalar_prefetch=2,
            grid=(kv_heads,),
            in_specs=in_specs,
            out_specs=out_specs,
            scratch_shapes=scratch,
        ),
        compiler_params=pltpu.CompilerParams(vmem_limit_bytes=56 * 2**20),
    )(place, older_count, queries, *arrays)


def project_kernel(steps, a_ref, w_ref, *out_refs):
    step = pl.program_id(0)
    product = jnp.dot(a_ref[...], w_ref[...], preferred_element_type=F32).astype(BF16)
    for n, out_ref in enumerate(out_refs):

        @pl.when((step >= n * steps) & (step < (n + 1) * steps))
        def _(out_ref=out_ref):
            out_ref[...] = product


def project(attended, weight, begin, columns, n_out, tile):
    rows, depth = attended.shape
    steps = columns // tile
    return pl.pallas_call(
        functools.partial(project_kernel, steps),
        out_shape=[jax.ShapeDtypeStruct((rows, columns), BF16)] * n_out,
        grid=(n_out * steps,),
        in_specs=[
            pl.BlockSpec((rows, depth), lambda i: (0, 0)),
            pl.BlockSpec((depth, tile), lambda i: (0, begin // tile + i)),
        ],
        out_specs=[
            pl.BlockSpec((rows, tile), lambda i, n=n: (0, jnp.clip(i - n * steps, 0, steps - 1))) for n in range(n_out)
        ],
        compiler_params=pltpu.CompilerParams(vmem_limit_bytes=40 * 2**20),
    )(attended, weight)


def combine_kernel(n_part, place, noise_step, gate_ref, residual_ref, *rest):
    gate = gate_ref[pl.ds(noise_step[place[1]], 1), :]
    total = rest[0][...].astype(F32)
    for part in rest[1:n_part]:
        total = total + part[...].astype(F32)
    rest[-1][...] = (residual_ref[...].astype(F32) + gate * total).astype(BF16)


def combine(place, noise_step, gate_table, residual, kept, kept_begin, parts, begin, columns, tile, out):
    rows, width = residual.shape
    here = pl.BlockSpec((rows, tile), lambda i, p, n: (0, begin // tile + i))
    in_specs = [pl.BlockSpec((gate_table.shape[0], tile), lambda i, p, n: (0, begin // tile + i)), here]
    in_specs += [pl.BlockSpec((rows, tile), lambda i, p, n: (0, kept_begin // tile + i))]
    in_specs += [pl.BlockSpec((rows, tile), lambda i, p, n: (0, i))] * len(parts)
    arguments = [place, noise_step, gate_table, residual, kept, *parts]
    aliases = {}
    if out is not None:
        aliases = {len(arguments): 0}
        in_specs.append(pl.BlockSpec(memory_space=pl.ANY))
        arguments.append(out)
    return pl.pallas_call(
        functools.partial(combine_kernel, 1 + len(parts)),
        out_shape=jax.ShapeDtypeStruct((rows, width), BF16),
        grid_spec=pltpu.PrefetchScalarGridSpec(
            num_scalar_prefetch=2, grid=(columns // tile,), in_specs=in_specs, out_specs=here
        ),
        input_output_aliases=aliases,
        compiler_params=pltpu.CompilerParams(vmem_limit_bytes=40 * 2**20),
    )(*arguments)


def move(block, n_span, sends, target):
    route = [(i, target(i)) for i in range(n_span) if sends(i) and 0 <= target(i) < n_span]
    return lax.ppermute(block, "span", route)


def on_device(
    queries,
    stacked_key_vectors,
    stacked_value_vectors,
    out_weight,
    residual,
    gate_table,
    noise_step,
    older_count,
):
    span_len = queries.shape[0]
    kv_heads = stacked_key_vectors.shape[1] // HEAD_SIZE
    group = queries.shape[1] // HEAD_SIZE // kv_heads
    model_width = out_weight.shape[1]
    n_span = lax.axis_size("span")
    n_head = lax.axis_size("head")
    my_span = lax.axis_index("span")
    my_head = lax.axis_index("head")
    rows = span_len // n_head

    tiles = stacked_value_vectors.reshape(span_len // HEAD_SIZE, HEAD_SIZE, kv_heads, HEAD_SIZE)
    own = jnp.stack([stacked_key_vectors, tiles.transpose(0, 3, 2, 1).reshape(stacked_value_vectors.shape)])
    hop = functools.partial(move, n_span=n_span)
    places = [jnp.stack([(my_head + k) % n_head, my_span]).astype(jnp.int32) for k in range(n_head)]

    chunk = model_width // 4

    def attend(k, blocks, state=None, columns=0, share=""):
        weight = out_weight if columns else None
        return attention(queries, places[k], older_count, rows, group, blocks, state, weight, columns, share)

    others = range(1, n_head)
    up = hop(own, sends=lambda i: True, target=lambda i: i + 4)
    across = hop(own, sends=lambda i: True, target=lambda i: i ^ 2)
    beside = hop(own, sends=lambda i: i & 1 == 0, target=lambda i: i ^ 1)
    states = [attend(k, {0: own}) for k in range(n_head)]
    up, across, beside, states = lax.optimization_barrier((up, across, beside, states))
    across_up = hop(across, sends=lambda i: i & 2 == 0, target=lambda i: i + 4)
    up_across = hop(up, sends=lambda i: i & 2 == 0, target=lambda i: i ^ 2)
    up_diagonal = hop(up, sends=lambda i: i & 2 > 0, target=lambda i: i + 2)
    up_seventh = hop(up, sends=lambda i: i & 1 > 0, target=lambda i: i + 3)
    across_beside = hop(across, sends=lambda i: i & 2 > 0, target=lambda i: i ^ 1)
    up_beside = hop(up, sends=lambda i: True, target=lambda i: i ^ 1)
    early = {1: beside, 2: across, 3: across_beside, 4: up, 5: up_beside}
    for k in others:
        states[k] = attend(k, early, states[k])
    states[0] = attend(0, early, states[0], share="begin")
    across_up, up_across, up_diagonal, up_seventh, states = lax.optimization_barrier(
        (across_up, up_across, up_diagonal, up_seventh, states)
    )
    across_up_beside = hop(across_up, sends=lambda i: i & 2 == 0, target=lambda i: i ^ 1)
    up_across_beside = hop(up_across, sends=lambda i: i & 2 > 0, target=lambda i: i ^ 1)
    up_diagonal_beside = hop(up_diagonal, sends=lambda i: i & 2 == 0, target=lambda i: i ^ 1)
    late = {
        6: across_up,
        7: across_up_beside,
        8: up_across,
        9: up_across_beside,
        10: up_seventh,
        11: up_diagonal,
        12: up_diagonal_beside,
    }

    received = []
    for k in others:
        attended, partial = attend(k, late, states[k], chunk)
        route = [(i, (i + k) % n_head) for i in range(n_head)]
        begun = lax.ppermute(partial, "head", route)
        partials = project(attended, out_weight, chunk, chunk, 3, chunk)
        received.append([begun] + [lax.ppermute(partial, "head", route) for partial in partials])

    states, attended = lax.optimization_barrier((states, attended))
    attended, kept = attend(0, {**early, **late}, states[0], 3 * chunk, share="end")
    (kept_end,) = project(attended, out_weight, 3 * chunk, chunk, 1, chunk // 2)
    out = None
    for c in range(4):
        parts = [got[c] for got in received]
        at = (kept, c * chunk) if c < 3 else (kept_end, 0)
        out = combine(places[0], noise_step, gate_table, residual, *at, parts, c * chunk, chunk, chunk // 2, out)
    return out


def solution(mesh):
    in_specs = (
        P("span", "head"),
        P("span", "head"),
        P("span", "head"),
        P("head", None),
        P(("span", "head"), None),
        P(),
        P(),
        P(),
    )
    out_specs = P(("span", "head"), None)
    return jax.shard_map(
        on_device, mesh=mesh, in_specs=in_specs, out_specs=out_specs, check_vma=False
    )
```
